32 devices in a mesh: grp: 2 (over x), tm: 16 (over z, y, core).
Axes of the slice: x: 2, y: 2, z: 4, core: 2. Of those that a mesh axis runs over, the one named last changes fastest.
Arguments:
- old_start: float32 [32, 69, 8, 128], P(('grp', 'tm')), parts along dimension 0, may hold values from -6 to 6
- weight_in: bfloat16 [621, 256], replicated, may hold values from -0.25 to 0.25
- weight_mid: bfloat16 [2304, 256], replicated, may hold values from -0.125 to 0.125
- weight_out: bfloat16 [69, 2304], replicated, may hold values from -0.125 to 0.125
- tendency: float32 [69, 69], replicated, may hold values from -0.0078125 to 0.0078125, as said below
Outputs:
- new_start: float32 [32, 69, 8, 128], P(('grp', 'tm')), parts along dimension 0
- correction_size: float32 [138], P('grp'), parts along dimension 0
The draws below stay inside these ranges and needn't reach their ends.
There are 2 independent parts, one for each index of `grp`. The reference program is written for one: setup_inputs(seed, part) draws one part's arguments, and reference() takes and returns one part's arrays. A program takes and returns all parts, laid end to end along the dimension named above; an argument that names none is the same for every part. Nothing has to cross between parts.
Inputs may be any that keep to these rules, and one draw needn't show every extreme that they name: `tendency`: entries of the coupling matrix.
All inputs are finite; a program needn't handle non-finite values.
Results may differ from the reference program's by a relative error of at most 0.0023.
Values sent between devices are 32-bit elements; how exact they have to be, the bound alone decides.
A program may use at most 128 MiB of HBM per device.

```python
import jax
import jax.numpy as jnp
from jax import lax

FIELDS = 69
CH = 256
ROWS = 8
LON = 128
FINE = 2
SLICES = 16


def draw_tendency(key, part):
    key = jax.random.fold_in(key, 11)
    key_main, key_rest = jax.random.split(key)
    shape = (FIELDS, FIELDS)
    entries = 2.0 * jax.random.bernoulli(key_main, 0.5, shape).astype(jnp.float32) - 1.0
    upper = jnp.triu(entries, 1)
    rotation = 0.007 * (upper - upper.T)
    general = jax.random.uniform(key_rest, shape, jnp.float32, -0.0008, 0.0008)
    return (rotation + general).astype(jnp.float32)


def shard_levels(stream_key, dims, cuts, smallest, high):
    def one(axis_at, blocks):
        steps = jax.random.uniform(jax.random.fold_in(jax.random.fold_in(stream_key, 6), axis_at), (blocks,), jnp.float32, smallest / len(cuts), high / len(cuts))
        return jnp.repeat(jnp.exp(steps), dims[axis_at] // blocks).reshape((-1,) + (1,) * (len(dims) - axis_at - 1))

    gain = one(*cuts[0])
    for cut in cuts[1:]:
        gain = gain * one(*cut)
    return gain


def centred(key, dims, scale, limit, cuts=(), kind=jnp.bfloat16):
    values = scale * jax.random.normal(key, dims, jnp.float32)
    if cuts:
        values = values * shard_levels(key, dims, cuts, -0.22, 0.18)
    return jnp.clip(values, -limit, limit).astype(kind)


def setup_inputs(seed: int = 0, part: int = 0) -> dict:
    splits = jax.random.split(jax.random.key(seed), 6)
    part_splits = jax.random.split(jax.random.fold_in(splits[5], part), 6)
    old_start = centred(part_splits[0], (SLICES, FIELDS, ROWS, LON), 1.0, 6.0, ((0, 16),), jnp.float32)
    weight_in = centred(splits[1], (9 * FIELDS, CH), (9 * FIELDS) ** -0.5, 0.25)
    weight_mid = centred(splits[2], (9 * CH, CH), (9 * CH) ** -0.5, 0.125)
    weight_out = centred(splits[3], (FIELDS, 9 * CH), (9 * CH) ** -0.5, 0.125)
    tendency = draw_tendency(jax.random.fold_in(splits[5], 71), part)
    return dict(old_start=old_start, weight_in=weight_in, weight_mid=weight_mid, weight_out=weight_out, tendency=tendency)


DAMPING = 0.995

def patches(field):
    channels, rows, columns = field.shape
    wrapped = jnp.concatenate([field[:, :, -1:], field, field[:, :, :1]], axis=2)
    zero_row = jnp.zeros((channels, 1, columns + 2), field.dtype)
    padded = jnp.concatenate([zero_row, wrapped, zero_row], axis=1)
    pieces = [padded[:, above:above + rows, left:left + columns] for above in range(3) for left in range(3)]
    return jnp.stack(pieces, axis=0).reshape(9 * channels, rows * columns)

def conv_forward(field, kernel):
    channels, rows, columns = field.shape
    result = lax.dot_general(kernel, patches(field), (((0,), (0,)), ((), ())), preferred_element_type=jnp.float32)
    return result.reshape(kernel.shape[1], rows, columns)

def conv_back(field, kernel):
    channels, rows, columns = field.shape
    result = jnp.dot(kernel, patches(field), preferred_element_type=jnp.float32)
    return result.reshape(kernel.shape[0], rows, columns)

def propagate(current, weight_in, weight_mid, weight_out):
    for _ in range(FINE):
        hidden_one = jax.nn.silu(conv_forward(current.astype(jnp.bfloat16), weight_in)).astype(jnp.bfloat16)
        hidden_two = jax.nn.silu(conv_forward(hidden_one, weight_mid)).astype(jnp.bfloat16)
        current = current + conv_back(hidden_two, weight_out)
    return current

def coarse_map(current, tendency):
    flat = current.reshape(current.shape[0], -1)
    mixed = jnp.dot(tendency, flat, precision=lax.Precision.HIGHEST)
    return DAMPING * current + mixed.reshape(current.shape)

def reference(old_start, weight_in, weight_mid, weight_out, tendency):
    fine_end = lax.map(lambda current: propagate(current, weight_in, weight_mid, weight_out), old_start)

    def advance(current, inputs_pair):
        fine_piece, old_piece = inputs_pair
        following = coarse_map(current, tendency) + fine_piece - coarse_map(old_piece, tendency)
        return (following, following)
    _, later = lax.scan(advance, old_start[0], (fine_end[:-1], old_start[:-1]))
    new_start = jnp.concatenate([old_start[:1], later], axis=0)
    change = new_start - old_start
    mean_square = lax.optimization_barrier(jnp.sum(change * change, axis=(0, 2, 3))) / (old_start.shape[0] * old_start.shape[2] * old_start.shape[3])
    correction_size = jnp.sqrt(mean_square + 1e-06)
    return (new_start, correction_size)
```

```python
import functools

import jax
import jax.numpy as jnp
from jax import lax
from jax.experimental import pallas as pl
from jax.experimental.pallas import tpu as pltpu
from jax.sharding import PartitionSpec as P

FINE = 2
DAMPING = 0.995
MESH = pl.DeviceIdType.MESH
HIGHEST = lax.Precision.HIGHEST
F32 = jnp.float32
BF16 = jnp.bfloat16

FP = 72
FK = 80


def exact(a, b):
    return jnp.dot(a, b, precision=HIGHEST, preferred_element_type=F32)


def silu(x):
    return 0.5 * x * (1.0 + jnp.tanh(0.5 * x))


def coarse_matrix(ten_ref, mat):
    fields = ten_ref.shape[0]
    mat[...] = jnp.zeros_like(mat)
    mat[0:fields, 0:fields] = ten_ref[...]
    across = lax.broadcasted_iota(jnp.int32, (FP, FP), 0)
    down = lax.broadcasted_iota(jnp.int32, (FP, FP), 1)
    return mat[:, 0:FP] + jnp.where(across == down, DAMPING, 0.0).astype(F32)


def network(u_ref, win_ref, wmid_ref, wout_ref, ten_ref, f_ref, cur, mat, wtall, wi, wo, xt, acc, hcat, h2):
    fields = ten_ref.shape[0]
    ch = win_ref.shape[1]
    rows = cur.shape[0]
    lon = cur.shape[2]
    cells = rows * lon
    wtall[0 : 9 * fields] = win_ref[...].astype(F32)
    wtall[9 * fields :] = jnp.zeros((wtall.shape[0] - 9 * fields, ch), F32)
    wi[...] = jnp.zeros_like(wi)
    wo[...] = jnp.zeros_like(wo)
    for a in range(3):
        for b in range(3):
            t = 3 * a + b
            wi[a, b * FK : (b + 1) * FK] = wtall[t * fields : t * fields + FK].astype(BF16)
            wo[a, b * FK : b * FK + fields] = wout_ref[:, t * ch : (t + 1) * ch]
    cur[...] = jnp.zeros_like(cur)
    for r in range(rows):
        cur[r, 0:fields] = u_ref[pl.ds(r, fields, stride=rows), :]
    for pad in (xt, hcat, h2):
        pad[0:lon] = jnp.zeros((lon, pad.shape[1]), BF16)
        pad[lon + cells :] = jnp.zeros((lon, pad.shape[1]), BF16)

    for _ in range(FINE):
        for r in range(rows):
            x = cur[r]
            wide = jnp.concatenate(
                [pltpu.roll(x, 1, 1), x, pltpu.roll(x, lon - 1, 1), jnp.zeros((xt.shape[1] - 3 * FK, lon), F32)], axis=0
            )
            xt[(r + 1) * lon : (r + 2) * lon] = wide.T.astype(BF16)
        acc[...] = sum(
            jnp.dot(xt[a * lon : a * lon + cells], wi[a], preferred_element_type=F32) for a in range(3)
        )
        for r in range(rows):
            h = silu(acc[r * lon : (r + 1) * lon])
            here = slice((r + 1) * lon, (r + 2) * lon)
            hcat[here, 0:ch] = pltpu.roll(h, 1, 0).astype(BF16)
            hcat[here, ch : 2 * ch] = h.astype(BF16)
            hcat[here, 2 * ch : 3 * ch] = pltpu.roll(h, lon - 1, 0).astype(BF16)
        acc[...] = sum(
            jnp.dot(
                hcat[a * lon : a * lon + cells],
                wmid_ref[a * 3 * ch : (a + 1) * 3 * ch],
                preferred_element_type=F32,
            )
            for a in range(3)
        )
        for r in range(rows):
            h2[(r + 1) * lon : (r + 2) * lon] = silu(acc[r * lon : (r + 1) * lon]).astype(BF16)
        y = sum(
            lax.dot_general(
                wo[a], h2[a * lon : a * lon + cells], (((1,), (1,)), ((), ())), preferred_element_type=F32
            )
            for a in range(3)
        )
        for r in range(rows):
            part = y[:, r * lon : (r + 1) * lon]
            cur[r] = (
                cur[r]
                + part[FK : 2 * FK]
                + pltpu.roll(part[0:FK], 1, 1)
                + pltpu.roll(part[2 * FK : 3 * FK], lon - 1, 1)
            )

    matrix = coarse_matrix(ten_ref, mat)
    later = jnp.where(lax.axis_index("tm") == 0, 0.0, 1.0).astype(F32)
    for q in range(rows // 2):
        fine = jnp.concatenate([cur[2 * q, 0:FP], cur[2 * q + 1, 0:FP]], axis=1)
        old = old_quarter(u_ref, q, fields, rows)
        f_ref[q] = fine - later * exact(matrix, old)


def old_quarter(u_ref, q, fields, rows):
    pair = [u_ref[pl.ds(2 * q + k, fields, stride=rows), :] for k in range(2)]
    flat = jnp.concatenate(pair, axis=1)
    return jnp.concatenate([flat, jnp.zeros((FP - fields, flat.shape[1]), F32)], axis=0)


def scan(n, u_ref, f_ref, ten_ref, new_ref, size_ref, mat, old, near, tot, cross, carry_in, carry_out, carry_side,
         give, keep, back, sq, sems_s, sems_r, sq_s, sq_r):
    fields = ten_ref.shape[0]
    rows = u_ref.shape[0] // fields
    me = lax.axis_index("tm")
    core = lax.rem(me, 2)
    side = lax.rem(me // 2, 2)
    block = me // 4
    blocks = n // 4
    mate = me + 1 - 2 * core
    other = me + 2 - 4 * side
    following = lax.rem(me + 4, n)
    previous = lax.rem(me + n - 4, n)

    barrier = pltpu.get_barrier_semaphore()

    @pl.loop(1, n)
    def _(d):
        pl.semaphore_signal(barrier, inc=1, device_id={"tm": lax.rem(me + d, n)}, device_id_type=MESH)

    pl.semaphore_wait(barrier, n - 1)

    def send(src, dst, k, to):
        return pltpu.make_async_remote_copy(
            src_ref=src, dst_ref=dst, send_sem=sems_s.at[k], recv_sem=sems_r.at[k], device_id={"tm": to}, device_id_type=MESH
        )

    first = [send(f_ref.at[2 * (1 - core) + k], near.at[k], k, mate) for k in range(2)]
    for copy in first:
        copy.start()

    a1 = coarse_matrix(ten_ref, mat)
    a2 = exact(a1, a1)
    a3 = exact(a2, a1)
    a4 = exact(a2, a2)
    for q in range(4):
        old[q] = old_quarter(u_ref, q, fields, rows)

    zero = jnp.zeros(near.shape[1:], F32)
    upper = core == 0
    for copy in first:
        copy.wait_recv()

    def early_late(k):
        mine, theirs = f_ref[2 * core + k], near[k]
        return jnp.where(upper, mine, theirs), jnp.where(upper, theirs, mine)

    for k, quarter in ((0, 1 - side), (1, side)):
        early, late = early_late(quarter)
        tot[k] = exact(a1, early) + late
        if k == 0:
            swap = send(tot.at[0], cross.at[0], 2, other)
            swap.start()
    extra = send(tot.at[1], cross.at[1], 3, other)

    @pl.when(side == 0)
    def _():
        extra.start()
        cross[1] = zero

    swap.wait_recv()
    low = jnp.where(side == 0, tot[1], cross[0])
    high = jnp.where(side == 0, cross[0], tot[1])
    plane = exact(a2, low) + high

    pass_on = send(carry_out, carry_in, 4, following)
    get = send(carry_out, carry_in, 4, previous)
    aside = send(carry_in, carry_side, 5, other)

    @pl.when(block == 0)
    def _():
        carry_in[...] = zero
        carry_side[...] = zero
        carry_out[...] = plane

    @pl.when(block > 0)
    def _():
        get.wait_recv()
        aside.start()
        carry_out[...] = exact(a4, carry_in[...]) + plane

    @pl.when(block < blocks - 1)
    def _():
        pass_on.start()

    @pl.when(side == 1)
    def _():
        extra.wait_recv()

    def results(quarter, carry, offset):
        early, _ = early_late(quarter)
        n0 = jnp.where(side == 0, carry, exact(a2, carry) + offset)
        n1 = exact(a1, n0) + early
        return n0, n1

    tasks = []
    for k in range(2):
        if k == 1:

            @pl.when(block > 0)
            def _():
                aside.wait_recv()

        quarter = side if k == 0 else 1 - side
        n0, n1 = results(quarter, carry_in[...] if k == 0 else carry_side[...], cross[k])
        give[k] = jnp.where(upper, n1, n0)
        keep[quarter] = jnp.where(upper, n0, n1)
        copy = send(give.at[k], back.at[k], 6 + k, mate)
        copy.start()
        tasks.append(copy)

    for copy in tasks:
        copy.wait_recv()

    start = me == 0
    total = jnp.zeros((8, FP), F32)
    ones = jnp.ones((8, near.shape[2]), F32)
    for h in range(2):
        for k in range(2):
            own = h == 0
            half = core if own else 1 - core
            quarter = 2 * half + k
            value = keep[k] if own else back[jnp.where(side == k, 0, 1)]
            before = old[quarter]
            value = jnp.where(start, before, value)
            change = value - before
            total = total + lax.dot_general(
                ones, change * change, (((1,), (1,)), ((), ())), precision=HIGHEST, preferred_element_type=F32
            )
            for j in range(2):
                new_ref[pl.ds(2 * quarter + j, fields, stride=rows), :] = value[0:fields, j * 128 : (j + 1) * 128]

    sq[me] = jnp.concatenate([total, jnp.zeros((8, 128 - FP), F32)], axis=1)

    def share(d):
        to = lax.rem(me + d, n)
        return pltpu.make_async_remote_copy(
            src_ref=sq.at[me], dst_ref=sq.at[me], send_sem=sq_s.at[to], recv_sem=sq_r.at[me], device_id={"tm": to},
            device_id_type=MESH,
        )

    def arrive(d):
        of = lax.rem(me + d, n)
        return pltpu.make_async_remote_copy(
            src_ref=sq.at[of], dst_ref=sq.at[of], send_sem=sq_s.at[of], recv_sem=sq_r.at[of], device_id={"tm": of},
            device_id_type=MESH,
        )

    @pl.loop(1, n)
    def _(d):
        share(d).start()

    @pl.loop(1, n)
    def _(d):
        arrive(d).wait_recv()

    everyone = jnp.sum(sq[...], axis=0)
    counted = n * rows * 128
    size_ref[...] = jnp.sqrt(everyone[0:1, 0:fields] / counted + 1e-06)

    @pl.loop(1, n)
    def _(d):
        share(d).wait_send()

    for copy in first + tasks + [swap]:
        copy.wait_send()

    @pl.when(side == 0)
    def _():
        extra.wait_send()

    @pl.when(block > 0)
    def _():
        aside.wait_send()

    @pl.when(block < blocks - 1)
    def _():
        pass_on.wait_send()


def per_device(n, old_start, weight_in, weight_mid, weight_out, tendency):
    _, fields, rows, lon = old_start.shape
    ch = weight_in.shape[1]
    cells = rows * lon
    wide = lon + cells + lon
    flat = old_start.reshape(fields * rows, lon)
    vmem = pl.BlockSpec(memory_space=pltpu.VMEM)
    quarter = (FP, 2 * lon)
    forcing = pl.pallas_call(
        network,
        out_shape=jax.ShapeDtypeStruct((4,) + quarter, F32),
        in_specs=[vmem] * 5,
        out_specs=vmem,
        scratch_shapes=[
            pltpu.VMEM((rows, FK, lon), F32),
            pltpu.VMEM((FP, 128), F32),
            pltpu.VMEM((640, ch), F32),
            pltpu.VMEM((3, 256, ch), BF16),
            pltpu.VMEM((3, 3 * FK, ch), BF16),
            pltpu.VMEM((wide, 256), BF16),
            pltpu.VMEM((cells, ch), F32),
            pltpu.VMEM((wide, 3 * ch), BF16),
            pltpu.VMEM((wide, ch), BF16),
        ],
        compiler_params=pltpu.CompilerParams(vmem_limit_bytes=40 * 2**20),
        name="network",
    )(flat, weight_in, weight_mid, weight_out, tendency)
    new, size = pl.pallas_call(
        functools.partial(scan, n),
        out_shape=(jax.ShapeDtypeStruct((fields * rows, lon), F32), jax.ShapeDtypeStruct((1, fields), F32)),
        in_specs=[vmem] * 3,
        out_specs=(vmem, vmem),
        scratch_shapes=[
            pltpu.VMEM((FP, 128), F32),
            pltpu.VMEM((4,) + quarter, F32),
            pltpu.VMEM((2,) + quarter, F32),
            pltpu.VMEM((2,) + quarter, F32),
            pltpu.VMEM((2,) + quarter, F32),
            pltpu.VMEM(quarter, F32),
            pltpu.VMEM(quarter, F32),
            pltpu.VMEM(quarter, F32),
            pltpu.VMEM((2,) + quarter, F32),
            pltpu.VMEM((2,) + quarter, F32),
            pltpu.VMEM((2,) + quarter, F32),
            pltpu.VMEM((n, 8, 128), F32),
            pltpu.SemaphoreType.DMA((8,)),
            pltpu.SemaphoreType.DMA((8,)),
            pltpu.SemaphoreType.DMA((n,)),
            pltpu.SemaphoreType.DMA((n,)),
        ],
        compiler_params=pltpu.CompilerParams(
            collective_id=0, has_side_effects=True, vmem_limit_bytes=24 * 2**20
        ),
        name="scan",
    )(flat, forcing, tendency)
    return (new.reshape(old_start.shape), size.reshape(fields))


def solution(mesh):
    in_specs = (P(("grp", "tm"), None, None, None), P(), P(), P(), P())
    out_specs = (P(("grp", "tm"), None, None, None), P("grp"))
    return jax.shard_map(
        functools.partial(per_device, mesh.shape["tm"]),
        mesh=mesh, in_specs=in_specs, out_specs=out_specs, check_vma=False,
    )
```

```python
import functools

import jax
import jax.numpy as jnp
from jax import lax
from jax.experimental import pallas as pl
from jax.experimental.pallas import tpu as pltpu
from jax.sharding import PartitionSpec as P

FINE = 2
DAMPING = 0.995
MESH = pl.DeviceIdType.MESH
HIGHEST = lax.Precision.HIGHEST
F32 = jnp.float32
BF16 = jnp.bfloat16

FP = 72
FK = 80


def exact(a, b):
    return jnp.dot(a, b, precision=HIGHEST, preferred_element_type=F32)


def silu(x):
    return 0.5 * x * (1.0 + jnp.tanh(0.5 * x))


def coarse_matrix(ten_ref, mat):
    fields = ten_ref.shape[0]
    mat[...] = jnp.zeros_like(mat)
    mat[0:fields, 0:fields] = ten_ref[...]
    across = lax.broadcasted_iota(jnp.int32, (FP, FP), 0)
    down = lax.broadcasted_iota(jnp.int32, (FP, FP), 1)
    return mat[:, 0:FP] + jnp.where(across == down, DAMPING, 0.0).astype(F32)


def program(n, u_hbm, win_hbm, wmid_hbm, wout_hbm, ten_hbm, new_hbm, size_ref,
            u_ref, win_ref, wmid_ref, wout_ref, ten_ref, new_ref,
            cur, mat, wtall, wi, wo, xt, acc, hcat, h2,
            old, old_mate, force, near, pair, gather, carry, ahead, give, keep, back, sq,
            load, store, old_s, old_r, near_s, near_r, pair_s, pair_r, carry_s, carry_r, back_s, back_r, sq_s, sq_r):
    fields = ten_ref.shape[0]
    ch = win_ref.shape[1]
    rows, _, lon = cur.shape
    cells = rows * lon
    half = rows // 2
    chips = n // 2
    me = lax.axis_index("tm")
    core = lax.rem(me, 2)
    chip = me // 2
    mate = me + 1 - 2 * core
    upper = core == 0

    loads = [
        pltpu.make_async_copy(src, dst, load.at[k])
        for k, (src, dst) in enumerate(
            ((win_hbm, win_ref), (u_hbm, u_ref), (wout_hbm, wout_ref), (ten_hbm, ten_ref), (wmid_hbm, wmid_ref))
        )
    ]
    for copy in loads:
        copy.start()
    barrier = pltpu.get_barrier_semaphore()

    @pl.loop(1, n)
    def _(d):
        pl.semaphore_signal(barrier, inc=1, device_id={"tm": lax.rem(me + d, n)}, device_id_type=MESH)

    def send(src, dst, sent, got, to):
        return pltpu.make_async_remote_copy(
            src_ref=src, dst_ref=dst, send_sem=sent, recv_sem=got, device_id={"tm": to}, device_id_type=MESH
        )

    wi[...] = jnp.zeros_like(wi)
    wo[...] = jnp.zeros_like(wo)
    cur[...] = jnp.zeros_like(cur)
    for pad in (xt, hcat, h2):
        pad[0:lon] = jnp.zeros((lon, pad.shape[1]), BF16)
        pad[lon + cells :] = jnp.zeros((lon, pad.shape[1]), BF16)
    wtall[9 * fields :] = jnp.zeros((wtall.shape[0] - 9 * fields, ch), F32)
    loads[0].wait()
    wtall[0 : 9 * fields] = win_ref[...].astype(F32)
    for t in range(9):
        a, b = divmod(t, 3)
        wi[a, b * FK : (b + 1) * FK] = wtall[t * fields : t * fields + FK].astype(BF16)
    loads[1].wait()
    for r in range(rows):
        cur[r, 0:fields] = u_ref[pl.ds(r, fields, stride=rows), :]
        old[r] = cur[r, 0:FP]
    loads[2].wait()
    for t in range(9):
        a, b = divmod(t, 3)
        wo[a, b * FK : b * FK + fields] = wout_ref[:, t * ch : (t + 1) * ch]
    loads[3].wait()
    a1 = coarse_matrix(ten_ref, mat)
    a2 = exact(a1, a1)
    moved = jnp.where(me == 0, 0.0, 1.0).astype(F32)

    for step in range(FINE):
        for r in range(rows):
            x = cur[r]
            wide = jnp.concatenate(
                [pltpu.roll(x, 1, 1), x, pltpu.roll(x, lon - 1, 1), jnp.zeros((xt.shape[1] - 3 * FK, lon), F32)], axis=0
            )
            xt[(r + 1) * lon : (r + 2) * lon] = wide.T.astype(BF16)
        acc[...] = sum(
            jnp.dot(xt[a * lon : a * lon + cells], wi[a], preferred_element_type=F32) for a in range(3)
        )
        for r in range(rows):
            h = silu(acc[r * lon : (r + 1) * lon])
            here = slice((r + 1) * lon, (r + 2) * lon)
            hcat[here, 0:ch] = pltpu.roll(h, 1, 0).astype(BF16)
            hcat[here, ch : 2 * ch] = h.astype(BF16)
            hcat[here, 2 * ch : 3 * ch] = pltpu.roll(h, lon - 1, 0).astype(BF16)
        if step == 0:
            loads[4].wait()
        acc[...] = sum(
            jnp.dot(
                hcat[a * lon : a * lon + cells],
                wmid_ref[a * 3 * ch : (a + 1) * 3 * ch],
                preferred_element_type=F32,
            )
            for a in range(3)
        )
        for r in range(rows):
            h2[(r + 1) * lon : (r + 2) * lon] = silu(acc[r * lon : (r + 1) * lon]).astype(BF16)
        for part in (1 - core, core):
            first = part * half
            y = sum(
                lax.dot_general(
                    wo[a],
                    h2[pl.ds(pl.multiple_of((first + a) * lon, lon), half * lon), :],
                    (((1,), (1,)), ((), ())),
                    preferred_element_type=F32,
                )
                for a in range(3)
            )
            for k in range(half):
                piece = y[:, k * lon : (k + 1) * lon]
                cur[first + k] = (
                    cur[first + k]
                    + piece[FK : 2 * FK]
                    + pltpu.roll(piece[0:FK], 1, 1)
                    + pltpu.roll(piece[2 * FK : 3 * FK], lon - 1, 1)
                )
            if step == FINE - 1:
                before = jnp.concatenate([old[first + k] for k in range(half)], axis=1)
                mapped = moved * exact(a1, before)
                for k in range(half):
                    force[first + k] = cur[first + k, 0:FP] - mapped[:, k * lon : (k + 1) * lon]
                if part is not core:
                    to_mate = send(force.at[pl.ds(first, half)], near, near_s, near_r, mate)
                    to_mate.start()
        if step == 0:
            pl.semaphore_wait(barrier, n - 1)
            olds = send(old.at[pl.ds((1 - core) * half, half)], old_mate, old_s, old_r, mate)
            olds.start()

    mine = core * half
    base = chips // 2 - half // 2
    place = chip - base
    owner = jnp.logical_and(place >= 0, place < half)
    place = jnp.clip(place, 0, half - 1)

    to_mate.wait_recv()
    early = jnp.concatenate([jnp.where(upper, force[mine + k], near[k]) for k in range(half)], axis=1)
    mixed = exact(a1, early)
    gives = [
        send(pair.at[k], gather.at[chip], pair_s.at[k], pair_r.at[chip], 2 * (base + k) + core) for k in range(half)
    ]
    for k in range(half):
        late = jnp.where(upper, near[k], force[mine + k])
        pair[k] = mixed[:, k * lon : (k + 1) * lon] + late

        @pl.when(jnp.logical_and(chip != base + k, chip != chips - 1))
        def _():
            gives[k].start()

    @pl.when(chip == 0)
    def _():
        carry[...] = jnp.zeros_like(carry)

    def onward(g):
        return send(ahead.at[g], carry.at[place], carry_s.at[g], carry_r.at[place], 2 * g + core)

    @pl.when(owner)
    def _():
        gather[chip] = pair[place]
        value = None
        for g in range(chips - 1):

            @pl.when(chip != g)
            def _():
                send(pair.at[0], gather.at[g], pair_s.at[0], pair_r.at[g], 2 * g + core).wait_recv()

            value = gather[g] if g == 0 else exact(a2, value) + gather[g]
            ahead[g + 1] = value

            @pl.when(chip != g + 1)
            def _():
                onward(g + 1).start()

            @pl.when(chip == g + 1)
            def _():
                carry[place] = ahead[g + 1]

    olds.wait_recv()
    squares = jnp.zeros((FP, lon), F32)
    returns = []
    for k in range(half):

        @pl.when(jnp.logical_and(chip != 0, chip != base + k))
        def _():
            send(pair.at[0], carry.at[k], pair_s.at[0], carry_r.at[k], 2 * (base + k) + core).wait_recv()

        arrived = carry[k]
        mine_old, mate_old = old[mine + k], old_mate[k]
        n1 = exact(a1, arrived) + early[:, k * lon : (k + 1) * lon]
        n0 = jnp.where(chip == 0, jnp.where(upper, mine_old, mate_old), arrived)
        give[k] = jnp.where(upper, n1, n0)
        copy = send(give.at[k], back.at[k], back_s.at[k], back_r.at[k], mate)
        copy.start()
        returns.append(copy)
        kept = jnp.where(upper, n0, n1)
        keep[k] = kept
        d0, d1 = kept - mine_old, give[k] - mate_old
        squares = squares + (d0 * d0 + d1 * d1)

    total = lax.dot_general(
        jnp.ones((8, lon), F32), squares, (((1,), (1,)), ((), ())), precision=HIGHEST, preferred_element_type=F32
    )
    sq[me] = jnp.concatenate([total, jnp.zeros((8, lon - FP), F32)], axis=1)

    def share(d):
        to = lax.rem(me + d, n)
        return send(sq.at[me], sq.at[me], sq_s.at[to], sq_r.at[me], to)

    def arrive(d):
        of = lax.rem(me + d, n)
        return send(sq.at[of], sq.at[of], sq_s.at[of], sq_r.at[of], of)

    @pl.loop(1, n)
    def _(d):
        share(d).start()

    for k in range(half):
        new_ref[pl.ds(mine + k, fields, stride=rows), :] = keep[k, 0:fields]
    for k in range(half):
        returns[k].wait_recv()
        new_ref[pl.ds(half - mine + k, fields, stride=rows), :] = back[k, 0:fields]
    out = pltpu.make_async_copy(new_ref, new_hbm, store)
    out.start()

    @pl.loop(1, n)
    def _(d):
        arrive(d).wait_recv()

    everyone = jnp.sum(sq[...], axis=0)
    size_ref[...] = jnp.sqrt(everyone[0:1, 0:fields] / (n * cells) + 1e-06)

    @pl.loop(1, n)
    def _(d):
        share(d).wait_send()

    for copy in [olds, to_mate] + returns:
        copy.wait_send()
    for k in range(half):

        @pl.when(jnp.logical_and(chip != base + k, chip != chips - 1))
        def _():
            gives[k].wait_send()

    @pl.when(owner)
    def _():
        for g in range(1, chips):

            @pl.when(chip != g)
            def _():
                onward(g).wait_send()

    out.wait()


def per_device(n, old_start, weight_in, weight_mid, weight_out, tendency):
    _, fields, rows, lon = old_start.shape
    ch = weight_in.shape[1]
    cells = rows * lon
    half = rows // 2
    wide = lon + cells + lon
    chips = n // 2
    flat = old_start.reshape(fields * rows, lon)
    args = (flat, weight_in, weight_mid, weight_out, tendency)
    hbm = pl.BlockSpec(memory_space=pl.ANY)
    dma = pltpu.SemaphoreType.DMA

    def state(*lead):
        return pltpu.VMEM(lead + (FP, lon), F32)

    new, size = pl.pallas_call(
        functools.partial(program, n),
        out_shape=(jax.ShapeDtypeStruct(flat.shape, F32), jax.ShapeDtypeStruct((1, fields), F32)),
        in_specs=[hbm] * 5,
        out_specs=(hbm, pl.BlockSpec(memory_space=pltpu.VMEM)),
        scratch_shapes=[pltpu.VMEM(a.shape, a.dtype) for a in args]
        + [
            pltpu.VMEM(flat.shape, F32),
            pltpu.VMEM((rows, FK, lon), F32),
            pltpu.VMEM((FP, 128), F32),
            pltpu.VMEM((640, ch), F32),
            pltpu.VMEM((3, 256, ch), BF16),
            pltpu.VMEM((3, 3 * FK, ch), BF16),
            pltpu.VMEM((wide, 256), BF16),
            pltpu.VMEM((cells, ch), F32),
            pltpu.VMEM((wide, 3 * ch), BF16),
            pltpu.VMEM((wide, ch), BF16),
            state(rows),
            state(half),
            state(rows),
            state(half),
            state(half),
            state(chips),
            state(half),
            state(chips),
            state(half),
            state(half),
            state(half),
            pltpu.VMEM((n, 8, 128), F32),
            dma((5,)),
            dma,
            dma,
            dma,
            dma,
            dma,
            dma((half,)),
            dma((chips,)),
            dma((chips,)),
            dma((half,)),
            dma((half,)),
            dma((half,)),
            dma((n,)),
            dma((n,)),
        ],
        compiler_params=pltpu.CompilerParams(
            collective_id=0, has_side_effects=True, vmem_limit_bytes=48 * 2**20
        ),
        name="parareal",
    )(*args)
    return (new.reshape(old_start.shape), size.reshape(fields))


def solution(mesh):
    in_specs = (P(("grp", "tm"), None, None, None), P(), P(), P(), P())
    out_specs = (P(("grp", "tm"), None, None, None), P("grp"))
    return jax.shard_map(
        functools.partial(per_device, mesh.shape["tm"]),
        mesh=mesh, in_specs=in_specs, out_specs=out_specs, check_vma=False,
    )
```

```python
import functools

import jax
import jax.numpy as jnp
from jax import lax
from jax.experimental import pallas as pl
from jax.experimental.pallas import tpu as pltpu
from jax.sharding import PartitionSpec as P

FINE = 2
DAMPING = 0.995
MESH = pl.DeviceIdType.MESH
HIGHEST = lax.Precision.HIGHEST
F32 = jnp.float32
BF16 = jnp.bfloat16

FP = 72
FK = 80


def exact(a, b):
    return jnp.dot(a, b, precision=HIGHEST, preferred_element_type=F32)


def silu(x):
    return 0.5 * x * (1.0 + jnp.tanh(0.5 * x))


def coarse_matrix(ten_ref, mat):
    fields = ten_ref.shape[0]
    mat[...] = jnp.zeros_like(mat)
    mat[0:fields, 0:fields] = ten_ref[...]
    across = lax.broadcasted_iota(jnp.int32, (FP, FP), 0)
    down = lax.broadcasted_iota(jnp.int32, (FP, FP), 1)
    return mat[:, 0:FP] + jnp.where(across == down, DAMPING, 0.0).astype(F32)


def each_other(n, act):
    if n <= 32:
        for d in range(1, n):
            act(d)
    else:
        pl.loop(1, n)(act)


def program(n, u_hbm, win_hbm, wmid_hbm, wout_hbm, ten_hbm, new_hbm, size_ref,
            u_ref, win_ref, wmid_ref, wout_ref, ten_ref, new_ref,
            cur, mat, wtall, wi, wo, xt, acc, hcat, h2,
            old, old_mate, force, near, pair, gather, carry, ahead, give, keep, back, sq,
            load, store, old_s, old_r, near_s, near_r, pair_s, pair_r, carry_s, carry_r, back_s, back_r, sq_s, sq_r):
    fields = ten_ref.shape[0]
    ch = win_ref.shape[1]
    rows, _, lon = cur.shape
    cells = rows * lon
    half = rows // 2
    chips = n // 2
    me = lax.axis_index("tm")
    core = lax.rem(me, 2)
    chip = me // 2
    mate = me + 1 - 2 * core
    upper = core == 0

    loads = [
        pltpu.make_async_copy(src, dst, load.at[k])
        for k, (src, dst) in enumerate(
            ((win_hbm, win_ref), (u_hbm, u_ref), (wout_hbm, wout_ref), (ten_hbm, ten_ref), (wmid_hbm, wmid_ref))
        )
    ]
    for copy in loads:
        copy.start()
    barrier = pltpu.get_barrier_semaphore()

    def greet(d):
        pl.semaphore_signal(barrier, inc=1, device_id={"tm": lax.rem(me + d, n)}, device_id_type=MESH)

    each_other(n, greet)

    def send(src, dst, sent, got, to):
        return pltpu.make_async_remote_copy(
            src_ref=src, dst_ref=dst, send_sem=sent, recv_sem=got, device_id={"tm": to}, device_id_type=MESH
        )

    wi[...] = jnp.zeros_like(wi)
    wo[...] = jnp.zeros_like(wo)
    cur[...] = jnp.zeros_like(cur)
    for pad in (xt, hcat, h2):
        pad[0:lon] = jnp.zeros((lon, pad.shape[1]), BF16)
        pad[lon + cells :] = jnp.zeros((lon, pad.shape[1]), BF16)
    wtall[9 * fields :] = jnp.zeros((wtall.shape[0] - 9 * fields, ch), F32)
    loads[0].wait()
    wtall[0 : 9 * fields] = win_ref[...].astype(F32)
    for t in range(9):
        a, b = divmod(t, 3)
        wi[a, b * FK : (b + 1) * FK] = wtall[t * fields : t * fields + FK].astype(BF16)
    loads[1].wait()
    for r in range(rows):
        cur[r, 0:fields] = u_ref[pl.ds(r, fields, stride=rows), :]
        old[r] = cur[r, 0:FP]
    loads[2].wait()
    for t in range(9):
        a, b = divmod(t, 3)
        wo[a, b * FK : b * FK + fields] = wout_ref[:, t * ch : (t + 1) * ch]
    loads[3].wait()
    a1 = coarse_matrix(ten_ref, mat)
    a2 = exact(a1, a1)
    moved = jnp.where(me == 0, 0.0, 1.0).astype(F32)

    for step in range(FINE):
        for r in range(rows):
            x = cur[r]
            wide = jnp.concatenate(
                [pltpu.roll(x, 1, 1), x, pltpu.roll(x, lon - 1, 1), jnp.zeros((xt.shape[1] - 3 * FK, lon), F32)], axis=0
            )
            xt[(r + 1) * lon : (r + 2) * lon] = wide.T.astype(BF16)
        acc[...] = sum(
            jnp.dot(xt[a * lon : a * lon + cells], wi[a], preferred_element_type=F32) for a in range(3)
        )
        for r in range(rows):
            h = silu(acc[r * lon : (r + 1) * lon])
            here = slice((r + 1) * lon, (r + 2) * lon)
            hcat[here, 0:ch] = pltpu.roll(h, 1, 0).astype(BF16)
            hcat[here, ch : 2 * ch] = h.astype(BF16)
            hcat[here, 2 * ch : 3 * ch] = pltpu.roll(h, lon - 1, 0).astype(BF16)
        if step == 0:
            loads[4].wait()
        acc[...] = sum(
            jnp.dot(
                hcat[a * lon : a * lon + cells],
                wmid_ref[a * 3 * ch : (a + 1) * 3 * ch],
                preferred_element_type=F32,
            )
            for a in range(3)
        )
        for r in range(rows):
            h2[(r + 1) * lon : (r + 2) * lon] = silu(acc[r * lon : (r + 1) * lon]).astype(BF16)
        for part in (1 - core, core):
            first = part * half
            y = sum(
                lax.dot_general(
                    wo[a],
                    h2[pl.ds(pl.multiple_of((first + a) * lon, lon), half * lon), :],
                    (((1,), (1,)), ((), ())),
                    preferred_element_type=F32,
                )
                for a in range(3)
            )
            for k in range(half):
                piece = y[:, k * lon : (k + 1) * lon]
                cur[first + k] = (
                    cur[first + k]
                    + piece[FK : 2 * FK]
                    + pltpu.roll(piece[0:FK], 1, 1)
                    + pltpu.roll(piece[2 * FK : 3 * FK], lon - 1, 1)
                )
            if step == FINE - 1:
                before = jnp.concatenate([old[first + k] for k in range(half)], axis=1)
                mapped = moved * exact(a1, before)
                for k in range(half):
                    force[first + k] = cur[first + k, 0:FP] - mapped[:, k * lon : (k + 1) * lon]
                if part is not core:
                    to_mate = send(force.at[pl.ds(first, half)], near, near_s, near_r, mate)
                    to_mate.start()
        if step == 0:
            pl.semaphore_wait(barrier, n - 1)
            olds = send(old.at[pl.ds((1 - core) * half, half)], old_mate, old_s, old_r, mate)
            olds.start()

    mine = core * half
    base = chips // 2 - half // 2
    place = chip - base
    owner = jnp.logical_and(place >= 0, place < half)
    place = jnp.clip(place, 0, half - 1)

    to_mate.wait_recv()
    early = jnp.concatenate([jnp.where(upper, force[mine + k], near[k]) for k in range(half)], axis=1)
    mixed = exact(a1, early)
    gives = [
        send(pair.at[k], gather.at[chip], pair_s.at[k], pair_r.at[chip], 2 * (base + k) + core) for k in range(half)
    ]
    for k in range(half):
        late = jnp.where(upper, near[k], force[mine + k])
        pair[k] = mixed[:, k * lon : (k + 1) * lon] + late

        @pl.when(jnp.logical_and(chip != base + k, chip != chips - 1))
        def _():
            gives[k].start()

    @pl.when(chip == 0)
    def _():
        carry[...] = jnp.zeros_like(carry)

    def onward(g):
        return send(ahead.at[g], carry.at[place], carry_s.at[g], carry_r.at[place], 2 * g + core)

    @pl.when(owner)
    def _():
        gather[chip] = pair[place]
        value = None
        for g in range(chips - 1):

            @pl.when(chip != g)
            def _():
                send(pair.at[0], gather.at[g], pair_s.at[0], pair_r.at[g], 2 * g + core).wait_recv()

            value = gather[g] if g == 0 else exact(a2, value) + gather[g]
            ahead[g + 1] = value

            @pl.when(chip != g + 1)
            def _():
                onward(g + 1).start()

            @pl.when(chip == g + 1)
            def _():
                carry[place] = ahead[g + 1]

    olds.wait_recv()
    squares = jnp.zeros((FP, lon), F32)
    returns = []
    for k in range(half):

        @pl.when(jnp.logical_and(chip != 0, chip != base + k))
        def _():
            send(pair.at[0], carry.at[k], pair_s.at[0], carry_r.at[k], 2 * (base + k) + core).wait_recv()

        arrived = carry[k]
        mine_old, mate_old = old[mine + k], old_mate[k]
        n1 = exact(a1, arrived) + early[:, k * lon : (k + 1) * lon]
        n0 = jnp.where(chip == 0, jnp.where(upper, mine_old, mate_old), arrived)
        give[k] = jnp.where(upper, n1, n0)
        copy = send(give.at[k], back.at[k], back_s.at[k], back_r.at[k], mate)
        copy.start()
        returns.append(copy)
        kept = jnp.where(upper, n0, n1)
        keep[k] = kept
        d0, d1 = kept - mine_old, give[k] - mate_old
        squares = squares + (d0 * d0 + d1 * d1)

    total = lax.dot_general(
        jnp.ones((8, lon), F32), squares, (((1,), (1,)), ((), ())), precision=HIGHEST, preferred_element_type=F32
    )
    sq[me] = jnp.concatenate([total, jnp.zeros((8, lon - FP), F32)], axis=1)

    def share(d):
        to = lax.rem(me + d, n)
        return send(sq.at[me], sq.at[me], sq_s.at[to], sq_r.at[me], to)

    def arrive(d):
        of = lax.rem(me + d, n)
        return send(sq.at[of], sq.at[of], sq_s.at[of], sq_r.at[of], of)

    each_other(n, lambda d: share(d).start())

    for k in range(half):
        new_ref[pl.ds(mine + k, fields, stride=rows), :] = keep[k, 0:fields]
    for k in range(half):
        returns[k].wait_recv()
        new_ref[pl.ds(half - mine + k, fields, stride=rows), :] = back[k, 0:fields]
    out = pltpu.make_async_copy(new_ref, new_hbm, store)
    out.start()

    each_other(n, lambda d: arrive(d).wait_recv())

    everyone = jnp.sum(sq[...], axis=0)
    size_ref[...] = jnp.sqrt(everyone[0:1, 0:fields] / (n * cells) + 1e-06)

    each_other(n, lambda d: share(d).wait_send())

    for copy in [olds, to_mate] + returns:
        copy.wait_send()
    for k in range(half):

        @pl.when(jnp.logical_and(chip != base + k, chip != chips - 1))
        def _():
            gives[k].wait_send()

    @pl.when(owner)
    def _():
        for g in range(1, chips):

            @pl.when(chip != g)
            def _():
                onward(g).wait_send()

    out.wait()


def per_device(n, old_start, weight_in, weight_mid, weight_out, tendency):
    _, fields, rows, lon = old_start.shape
    ch = weight_in.shape[1]
    cells = rows * lon
    half = rows // 2
    wide = lon + cells + lon
    chips = n // 2
    flat = old_start.reshape(fields * rows, lon)
    args = (flat, weight_in, weight_mid, weight_out, tendency)
    hbm = pl.BlockSpec(memory_space=pl.ANY)
    dma = pltpu.SemaphoreType.DMA

    def state(*lead):
        return pltpu.VMEM(lead + (FP, lon), F32)

    new, size = pl.pallas_call(
        functools.partial(program, n),
        out_shape=(jax.ShapeDtypeStruct(flat.shape, F32), jax.ShapeDtypeStruct((1, fields), F32)),
        in_specs=[hbm] * 5,
        out_specs=(hbm, pl.BlockSpec(memory_space=pltpu.VMEM)),
        scratch_shapes=[pltpu.VMEM(a.shape, a.dtype) for a in args]
        + [
            pltpu.VMEM(flat.shape, F32),
            pltpu.VMEM((rows, FK, lon), F32),
            pltpu.VMEM((FP, 128), F32),
            pltpu.VMEM((640, ch), F32),
            pltpu.VMEM((3, 256, ch), BF16),
            pltpu.VMEM((3, 3 * FK, ch), BF16),
            pltpu.VMEM((wide, 256), BF16),
            pltpu.VMEM((cells, ch), F32),
            pltpu.VMEM((wide, 3 * ch), BF16),
            pltpu.VMEM((wide, ch), BF16),
            state(rows),
            state(half),
            state(rows),
            state(half),
            state(half),
            state(chips),
            state(half),
            state(chips),
            state(half),
            state(half),
            state(half),
            pltpu.VMEM((n, 8, 128), F32),
            dma((5,)),
            dma,
            dma,
            dma,
            dma,
            dma,
            dma((half,)),
            dma((chips,)),
            dma((chips,)),
            dma((half,)),
            dma((half,)),
            dma((half,)),
            dma((n,)),
            dma((n,)),
        ],
        compiler_params=pltpu.CompilerParams(
            collective_id=0, has_side_effects=True, vmem_limit_bytes=63 * 2**20
        ),
        name="parareal",
    )(*args)
    return (new.reshape(old_start.shape), size.reshape(fields))


def solution(mesh):
    in_specs = (P(("grp", "tm"), None, None, None), P(), P(), P(), P())
    out_specs = (P(("grp", "tm"), None, None, None), P("grp"))
    return jax.shard_map(
        functools.partial(per_device, mesh.shape["tm"]),
        mesh=mesh, in_specs=in_specs, out_specs=out_specs, check_vma=False,
    )
```

```python
import functools

import jax
import jax.numpy as jnp
from jax import lax
from jax.experimental import pallas as pl
from jax.experimental.pallas import tpu as pltpu
from jax.sharding import PartitionSpec as P

FINE = 2
DAMPING = 0.995
MESH = pl.DeviceIdType.MESH
HIGHEST = lax.Precision.HIGHEST
F32 = jnp.float32
BF16 = jnp.bfloat16

FP = 72
FK = 80
CHUNK = 256


def exact(a, b):
    return jnp.dot(a, b, precision=HIGHEST, preferred_element_type=F32)


def silu(x):
    return 0.5 * x * (1.0 + jnp.tanh(0.5 * x))


def coarse_matrix(ten_ref, mat):
    fields = ten_ref.shape[0]
    mat[...] = jnp.zeros_like(mat)
    mat[0:fields, 0:fields] = ten_ref[...]
    across = lax.broadcasted_iota(jnp.int32, (FP, FP), 0)
    down = lax.broadcasted_iota(jnp.int32, (FP, FP), 1)
    return mat[:, 0:FP] + jnp.where(across == down, DAMPING, 0.0).astype(F32)


def each_other(n, act):
    if n <= 32:
        for d in range(1, n):
            act(d)
    else:
        pl.loop(1, n)(act)


def program(n, u_hbm, win_hbm, wmid_hbm, wout_hbm, ten_hbm, new_hbm, size_ref,
            u_ref, win_ref, wmid_ref, wout_ref, ten_ref, new_ref,
            cur, mat, wtall, wi, wo, xt, hcat, h2,
            old, old_mate, force, near, pair, gather, carry, ahead, give, keep, back, sq,
            prior, priors, lead, leads, prior_s, prior_r, lead_s, lead_r, load, store, old_s, old_r, near_s, near_r, pair_s, pair_r, carry_s, carry_r, back_s, back_r, sq_s, sq_r):
    fields = ten_ref.shape[0]
    ch = win_ref.shape[1]
    rows, _, lon = cur.shape
    cells = rows * lon
    half = rows // 2
    chips = n // 2
    me = lax.axis_index("tm")
    core = lax.rem(me, 2)
    chip = me // 2
    mate = me + 1 - 2 * core
    upper = core == 0

    loads = [
        pltpu.make_async_copy(src, dst, load.at[k])
        for k, (src, dst) in enumerate(
            ((win_hbm, win_ref), (u_hbm, u_ref), (wout_hbm, wout_ref), (ten_hbm, ten_ref), (wmid_hbm, wmid_ref))
        )
    ]
    for copy in loads:
        copy.start()
    barrier = pltpu.get_barrier_semaphore()

    def greet(d):
        pl.semaphore_signal(barrier, inc=1, device_id={"tm": lax.rem(me + d, n)}, device_id_type=MESH)

    each_other(n, greet)

    def send(src, dst, sent, got, to):
        return pltpu.make_async_remote_copy(
            src_ref=src, dst_ref=dst, send_sem=sent, recv_sem=got, device_id={"tm": to}, device_id_type=MESH
        )

    mine = core * half
    base = chips // 2 - half // 2
    place = chip - base
    owner = jnp.logical_and(place >= 0, place < half)
    place = jnp.clip(place, 0, half - 1)

    def to_owner(src, dst, k, sent, got):
        return send(src.at[k], dst.at[chip], sent.at[k], got.at[chip], 2 * (base + k) + core)

    def from_chip(dst, g, got):
        return send(pair.at[0], dst.at[g], pair_s.at[0], got.at[g], 2 * g + core)

    wi[...] = jnp.zeros_like(wi)
    wo[...] = jnp.zeros_like(wo)
    cur[...] = jnp.zeros_like(cur)
    for pad in (xt, hcat, h2):
        pad[0:lon] = jnp.zeros((lon, pad.shape[1]), BF16)
        pad[lon + cells :] = jnp.zeros((lon, pad.shape[1]), BF16)
    wtall[9 * fields :] = jnp.zeros((wtall.shape[0] - 9 * fields, ch), F32)
    loads[0].wait()
    wtall[0 : 9 * fields] = win_ref[...].astype(F32)
    for t in range(9):
        a, b = divmod(t, 3)
        wi[a, b * FK : (b + 1) * FK] = wtall[t * fields : t * fields + FK].astype(BF16)
    loads[1].wait()
    for r in range(rows):
        cur[r, 0:fields] = u_ref[pl.ds(r, fields, stride=rows), :]
        old[r] = cur[r, 0:FP]
    loads[2].wait()
    for t in range(9):
        a, b = divmod(t, 3)
        wo[a, b * FK : b * FK + fields] = wout_ref[:, t * ch : (t + 1) * ch]
    loads[3].wait()
    a1 = coarse_matrix(ten_ref, mat)
    a2 = exact(a1, a1)
    moved = jnp.where(me == 0, 0.0, 1.0).astype(F32)

    for step in range(FINE):
        for r in range(rows):
            x = cur[r]
            wide = jnp.concatenate(
                [pltpu.roll(x, 1, 1), x, pltpu.roll(x, lon - 1, 1), jnp.zeros((xt.shape[1] - 3 * FK, lon), F32)], axis=0
            )
            xt[(r + 1) * lon : (r + 2) * lon] = wide.T.astype(BF16)
        for m in range(0, cells, CHUNK):
            wide = silu(
                sum(
                    jnp.dot(xt[m + a * lon : m + a * lon + CHUNK], wi[a], preferred_element_type=F32)
                    for a in range(3)
                )
            )
            for k in range(0, CHUNK, lon):
                h = wide[k : k + lon]
                here = slice(m + k + lon, m + k + 2 * lon)
                hcat[here, 0:ch] = pltpu.roll(h, 1, 0).astype(BF16)
                hcat[here, ch : 2 * ch] = h.astype(BF16)
                hcat[here, 2 * ch : 3 * ch] = pltpu.roll(h, lon - 1, 0).astype(BF16)
        if step == 0:
            loads[4].wait()
        if step == FINE - 1:
            olds.wait_recv()
            for k in range(half):
                prior[k] = jnp.where(upper, old[mine + k], old_mate[k])

                @pl.when(jnp.logical_and(chip != base + k, chip != 0))
                def _():
                    to_owner(prior, priors, k, prior_s, prior_r).start()

        for m in range(0, cells, CHUNK):
            h2[m + lon : m + lon + CHUNK] = silu(
                sum(
                    jnp.dot(
                        hcat[m + a * lon : m + a * lon + CHUNK],
                        wmid_ref[a * 3 * ch : (a + 1) * 3 * ch],
                        preferred_element_type=F32,
                    )
                    for a in range(3)
                )
            ).astype(BF16)
        for part in (1 - core, core):
            first = part * half
            y = sum(
                lax.dot_general(
                    wo[a],
                    h2[pl.ds(pl.multiple_of((first + a) * lon, lon), half * lon), :],
                    (((1,), (1,)), ((), ())),
                    preferred_element_type=F32,
                )
                for a in range(3)
            )
            for k in range(half):
                piece = y[:, k * lon : (k + 1) * lon]
                cur[first + k] = (
                    cur[first + k]
                    + piece[FK : 2 * FK]
                    + pltpu.roll(piece[0:FK], 1, 1)
                    + pltpu.roll(piece[2 * FK : 3 * FK], lon - 1, 1)
                )
            if step == FINE - 1:
                before = jnp.concatenate([old[first + k] for k in range(half)], axis=1)
                mapped = moved * exact(a1, before)
                for k in range(half):
                    force[first + k] = cur[first + k, 0:FP] - mapped[:, k * lon : (k + 1) * lon]
                if part is not core:
                    to_mate = send(force.at[pl.ds(first, half)], near, near_s, near_r, mate)
                    to_mate.start()
        if step == 0:
            pl.semaphore_wait(barrier, n - 1)
            olds = send(old.at[pl.ds((1 - core) * half, half)], old_mate, old_s, old_r, mate)
            olds.start()

    to_mate.wait_recv()
    early = jnp.concatenate([jnp.where(upper, force[mine + k], near[k]) for k in range(half)], axis=1)
    mixed = exact(a1, early)
    for k in range(half):
        late = jnp.where(upper, near[k], force[mine + k])
        pair[k] = mixed[:, k * lon : (k + 1) * lon] + late

        @pl.when(jnp.logical_and(chip != base + k, chip != chips - 1))
        def _():
            to_owner(pair, gather, k, pair_s, pair_r).start()

    for k in range(half):
        lead[k] = early[:, k * lon : (k + 1) * lon] - jnp.where(upper, old_mate[k], old[mine + k])

        @pl.when(chip != base + k)
        def _():
            to_owner(lead, leads, k, lead_s, lead_r).start()

    @pl.when(chip == 0)
    def _():
        carry[...] = jnp.zeros_like(carry)

    def onward(g):
        return send(ahead.at[g], carry.at[place], carry_s.at[g], carry_r.at[place], 2 * g + core)

    @pl.when(owner)
    def _():
        gather[chip] = pair[place]
        value = None
        for g in range(chips - 1):

            @pl.when(chip != g)
            def _():
                from_chip(gather, g, pair_r).wait_recv()

            value = gather[g] if g == 0 else exact(a2, value) + gather[g]
            ahead[g + 1] = value

            @pl.when(chip != g + 1)
            def _():
                onward(g + 1).start()

            @pl.when(chip == g + 1)
            def _():
                carry[place] = ahead[g + 1]

    slot = 2 * place + core

    def share(d):
        to = lax.rem(me + d, n)
        return send(sq.at[slot], sq.at[slot], sq_s.at[to], sq_r.at[slot], to)

    @pl.when(owner)
    def _():
        priors[chip] = prior[place]
        leads[chip] = lead[place]
        squares = jnp.zeros((FP, lon), F32)
        for g in range(chips):

            @pl.when(chip != g)
            def _():
                from_chip(leads, g, lead_r).wait_recv()

            change = leads[g]
            if g > 0:

                @pl.when(chip != g)
                def _():
                    from_chip(priors, g, prior_r).wait_recv()

                first_change = ahead[g] - priors[g]
                squares = squares + first_change * first_change
                change = change + exact(a1, ahead[g])
            squares = squares + change * change
        total = lax.dot_general(
            jnp.ones((8, lon), F32), squares, (((1,), (1,)), ((), ())), precision=HIGHEST, preferred_element_type=F32
        )
        sq[slot] = jnp.concatenate([total, jnp.zeros((8, lon - FP), F32)], axis=1)
        each_other(n, lambda d: share(d).start())

    returns = []
    for k in range(half):

        @pl.when(jnp.logical_and(chip != 0, chip != base + k))
        def _():
            send(pair.at[0], carry.at[k], pair_s.at[0], carry_r.at[k], 2 * (base + k) + core).wait_recv()

        arrived = carry[k]
        n1 = exact(a1, arrived) + early[:, k * lon : (k + 1) * lon]
        n0 = jnp.where(chip == 0, prior[k], arrived)
        give[k] = jnp.where(upper, n1, n0)
        copy = send(give.at[k], back.at[k], back_s.at[k], back_r.at[k], mate)
        copy.start()
        returns.append(copy)
        keep[k] = jnp.where(upper, n0, n1)

    for k in range(half):
        new_ref[pl.ds(mine + k, fields, stride=rows), :] = keep[k, 0:fields]
    for k in range(half):
        returns[k].wait_recv()
        new_ref[pl.ds(half - mine + k, fields, stride=rows), :] = back[k, 0:fields]
    out = pltpu.make_async_copy(new_ref, new_hbm, store)
    out.start()

    for other in range(2 * half):
        of = 2 * (base + other // 2) + other % 2

        @pl.when(me != of)
        def _():
            send(sq.at[other], sq.at[other], sq_s.at[of], sq_r.at[other], of).wait_recv()


    everyone = jnp.sum(sq[...], axis=0)
    size_ref[...] = jnp.sqrt(everyone[0:1, 0:fields] / (n * cells) + 1e-06)

    @pl.when(owner)
    def _():
        each_other(n, lambda d: share(d).wait_send())


    for copy in [olds, to_mate] + returns:
        copy.wait_send()
    for k in range(half):

        @pl.when(jnp.logical_and(chip != base + k, chip != chips - 1))
        def _():
            to_owner(pair, gather, k, pair_s, pair_r).wait_send()

        @pl.when(chip != base + k)
        def _():
            to_owner(lead, leads, k, lead_s, lead_r).wait_send()

        @pl.when(jnp.logical_and(chip != base + k, chip != 0))
        def _():
            to_owner(prior, priors, k, prior_s, prior_r).wait_send()

    @pl.when(owner)
    def _():
        for g in range(1, chips):

            @pl.when(chip != g)
            def _():
                onward(g).wait_send()

    out.wait()


def per_device(n, old_start, weight_in, weight_mid, weight_out, tendency):
    _, fields, rows, lon = old_start.shape
    ch = weight_in.shape[1]
    cells = rows * lon
    half = rows // 2
    wide = lon + cells + lon
    chips = n // 2
    flat = old_start.reshape(fields * rows, lon)
    args = (flat, weight_in, weight_mid, weight_out, tendency)
    hbm = pl.BlockSpec(memory_space=pl.ANY)
    dma = pltpu.SemaphoreType.DMA

    def state(*lead):
        return pltpu.VMEM(lead + (FP, lon), F32)

    new, size = pl.pallas_call(
        functools.partial(program, n),
        out_shape=(jax.ShapeDtypeStruct(flat.shape, F32), jax.ShapeDtypeStruct((1, fields), F32)),
        in_specs=[hbm] * 5,
        out_specs=(hbm, pl.BlockSpec(memory_space=pltpu.VMEM)),
        scratch_shapes=[pltpu.VMEM(a.shape, a.dtype) for a in args]
        + [
            pltpu.VMEM(flat.shape, F32),
            pltpu.VMEM((rows, FK, lon), F32),
            pltpu.VMEM((FP, 128), F32),
            pltpu.VMEM((640, ch), F32),
            pltpu.VMEM((3, 256, ch), BF16),
            pltpu.VMEM((3, 3 * FK, ch), BF16),
            pltpu.VMEM((wide, 256), BF16),
            pltpu.VMEM((wide, 3 * ch), BF16),
            pltpu.VMEM((wide, ch), BF16),
            state(rows),
            state(half),
            state(rows),
            state(half),
            state(half),
            state(chips),
            state(half),
            state(chips),
            state(half),
            state(half),
            state(half),
            pltpu.VMEM((2 * half, 8, lon), F32),
            state(half),
            state(chips),
            state(half),
            state(chips),
            dma((half,)),
            dma((chips,)),
            dma((half,)),
            dma((chips,)),
            dma((5,)),
            dma,
            dma,
            dma,
            dma,
            dma,
            dma((half,)),
            dma((chips,)),
            dma((chips,)),
            dma((half,)),
            dma((half,)),
            dma((half,)),
            dma((n,)),
            dma((2 * half,)),
        ],
        compiler_params=pltpu.CompilerParams(
            collective_id=0, has_side_effects=True, vmem_limit_bytes=63 * 2**20
        ),
        name="parareal",
    )(*args)
    return (new.reshape(old_start.shape), size.reshape(fields))


def solution(mesh):
    in_specs = (P(("grp", "tm"), None, None, None), P(), P(), P(), P())
    out_specs = (P(("grp", "tm"), None, None, None), P("grp"))
    return jax.shard_map(
        functools.partial(per_device, mesh.shape["tm"]),
        mesh=mesh, in_specs=in_specs, out_specs=out_specs, check_vma=False,
    )
```

```python
import functools

import jax
import jax.numpy as jnp
from jax import lax
from jax.experimental import pallas as pl
from jax.experimental.pallas import tpu as pltpu
from jax.sharding import PartitionSpec as P

FINE = 2
DAMPING = 0.995
MESH = pl.DeviceIdType.MESH
HIGHEST = lax.Precision.HIGHEST
F32 = jnp.float32
BF16 = jnp.bfloat16

FP = 72
FK = 80
CHUNK = 256


def exact(a, b):
    return jnp.dot(a, b, precision=HIGHEST, preferred_element_type=F32)


def silu(x):
    return 0.5 * x * (1.0 + jnp.tanh(0.5 * x))


def coarse_matrix(ten_ref, mat):
    fields = ten_ref.shape[0]
    mat[...] = jnp.zeros_like(mat)
    mat[0:fields, 0:fields] = ten_ref[...]
    across = lax.broadcasted_iota(jnp.int32, (FP, FP), 0)
    down = lax.broadcasted_iota(jnp.int32, (FP, FP), 1)
    return mat[:, 0:FP] + jnp.where(across == down, DAMPING, 0.0).astype(F32)


def each_other(n, act):
    if n <= 32:
        for d in range(1, n):
            act(d)
    else:
        pl.loop(1, n)(act)


def program(n, u_hbm, win_hbm, wmid_hbm, wout_hbm, ten_hbm, new_hbm, size_ref,
            u_ref, win_ref, wmid_ref, wout_ref, ten_ref, new_ref,
            cur, mat, wtall, wi, wo, xt, hcat, h2,
            old, old_mate, force, near, pair, gather, carry, ahead, give, keep, back, sq,
            prior, priors, lead, leads, prior_s, prior_r, lead_s, lead_r, load, store, old_s, old_r, near_s, near_r, pair_s, pair_r, carry_s, carry_r, back_s, back_r, sq_s, sq_r):
    fields = ten_ref.shape[0]
    ch = win_ref.shape[1]
    rows, _, lon = cur.shape
    cells = rows * lon
    half = rows // 2
    chips = n // 2
    me = lax.axis_index("tm")
    core = lax.rem(me, 2)
    chip = me // 2
    mate = me + 1 - 2 * core
    upper = core == 0

    loads = [
        pltpu.make_async_copy(src, dst, load.at[k])
        for k, (src, dst) in enumerate(
            ((win_hbm, win_ref), (u_hbm, u_ref), (wout_hbm, wout_ref), (ten_hbm, ten_ref), (wmid_hbm, wmid_ref))
        )
    ]
    for copy in loads:
        copy.start()
    barrier = pltpu.get_barrier_semaphore()

    def greet(d):
        pl.semaphore_signal(barrier, inc=1, device_id={"tm": lax.rem(me + d, n)}, device_id_type=MESH)

    each_other(n, greet)

    def send(src, dst, sent, got, to):
        return pltpu.make_async_remote_copy(
            src_ref=src, dst_ref=dst, send_sem=sent, recv_sem=got, device_id={"tm": to}, device_id_type=MESH
        )

    mine = core * half
    base = chips // 2 - half // 2
    place = chip - base
    owner = jnp.logical_and(place >= 0, place < half)
    place = jnp.clip(place, 0, half - 1)

    def to_owner(src, dst, k, sent, got):
        return send(src.at[k], dst.at[chip], sent.at[k], got.at[chip], 2 * (base + k) + core)

    def from_chip(dst, g, got):
        return send(pair.at[0], dst.at[g], pair_s.at[0], got.at[g], 2 * g + core)

    wi[...] = jnp.zeros_like(wi)
    wo[...] = jnp.zeros_like(wo)
    cur[...] = jnp.zeros_like(cur)
    for pad in (xt, hcat, h2):
        pad[0:lon] = jnp.zeros((lon, pad.shape[1]), BF16)
        pad[lon + cells :] = jnp.zeros((lon, pad.shape[1]), BF16)
    wtall[9 * fields :] = jnp.zeros((wtall.shape[0] - 9 * fields, ch), F32)
    loads[0].wait()
    wtall[0 : 9 * fields] = win_ref[...].astype(F32)
    for t in range(9):
        a, b = divmod(t, 3)
        wi[a, b * FK : (b + 1) * FK] = wtall[t * fields : t * fields + FK].astype(BF16)
    loads[1].wait()
    for r in range(rows):
        cur[r, 0:fields] = u_ref[pl.ds(r, fields, stride=rows), :]
        old[r] = cur[r, 0:FP]
    loads[2].wait()
    for t in range(9):
        a, b = divmod(t, 3)
        wo[a, b * FK : b * FK + fields] = wout_ref[:, t * ch : (t + 1) * ch]
    loads[3].wait()
    a1 = coarse_matrix(ten_ref, mat)
    a2 = exact(a1, a1)
    moved = jnp.where(me == 0, 0.0, 1.0).astype(F32)

    for step in range(FINE):
        for r in range(rows):
            x = cur[r]
            wide = jnp.concatenate(
                [pltpu.roll(x, 1, 1), x, pltpu.roll(x, lon - 1, 1), jnp.zeros((xt.shape[1] - 3 * FK, lon), F32)], axis=0
            )
            xt[(r + 1) * lon : (r + 2) * lon] = wide.T.astype(BF16)
        for m in range(0, cells, CHUNK):
            wide = silu(
                sum(
                    jnp.dot(xt[m + a * lon : m + a * lon + CHUNK], wi[a], preferred_element_type=F32)
                    for a in range(3)
                )
            )
            for k in range(0, CHUNK, lon):
                h = wide[k : k + lon]
                here = slice(m + k + lon, m + k + 2 * lon)
                hcat[here, 0:ch] = pltpu.roll(h, 1, 0).astype(BF16)
                hcat[here, ch : 2 * ch] = h.astype(BF16)
                hcat[here, 2 * ch : 3 * ch] = pltpu.roll(h, lon - 1, 0).astype(BF16)
        if step == 0:
            loads[4].wait()
        if step == FINE - 1:
            olds.wait_recv()
            for k in range(half):
                prior[k] = jnp.where(upper, old[mine + k], old_mate[k])

                @pl.when(jnp.logical_and(chip != base + k, chip != 0))
                def _():
                    to_owner(prior, priors, k, prior_s, prior_r).start()

        for m in range(0, cells, CHUNK):
            h2[m + lon : m + lon + CHUNK] = silu(
                sum(
                    jnp.dot(
                        hcat[m + a * lon : m + a * lon + CHUNK],
                        wmid_ref[a * 3 * ch : (a + 1) * 3 * ch],
                        preferred_element_type=F32,
                    )
                    for a in range(3)
                )
            ).astype(BF16)
        for part in (1 - core, core):
            first = part * half
            y = sum(
                lax.dot_general(
                    wo[a],
                    h2[pl.ds(pl.multiple_of((first + a) * lon, lon), half * lon), :],
                    (((1,), (1,)), ((), ())),
                    preferred_element_type=F32,
                )
                for a in range(3)
            )
            for k in range(half):
                piece = y[:, k * lon : (k + 1) * lon]
                cur[first + k] = (
                    cur[first + k]
                    + piece[FK : 2 * FK]
                    + pltpu.roll(piece[0:FK], 1, 1)
                    + pltpu.roll(piece[2 * FK : 3 * FK], lon - 1, 1)
                )
            if step == FINE - 1:
                before = jnp.concatenate([old[first + k] for k in range(half)], axis=1)
                mapped = moved * exact(a1, before)
                for k in range(half):
                    force[first + k] = cur[first + k, 0:FP] - mapped[:, k * lon : (k + 1) * lon]
                if part is not core:
                    to_mate = send(force.at[pl.ds(first, half)], near, near_s, near_r, mate)
                    to_mate.start()
        if step == 0:
            pl.semaphore_wait(barrier, n - 1)
            olds = send(old.at[pl.ds((1 - core) * half, half)], old_mate, old_s, old_r, mate)
            olds.start()

    to_mate.wait_recv()
    early = jnp.concatenate([jnp.where(upper, force[mine + k], near[k]) for k in range(half)], axis=1)
    mixed = exact(a1, early)
    for k in range(half):
        late = jnp.where(upper, near[k], force[mine + k])
        pair[k] = mixed[:, k * lon : (k + 1) * lon] + late

        @pl.when(jnp.logical_and(chip != base + k, chip != chips - 1))
        def _():
            to_owner(pair, gather, k, pair_s, pair_r).start()

    for k in range(half):
        lead[k] = early[:, k * lon : (k + 1) * lon] - jnp.where(upper, old_mate[k], old[mine + k])

        @pl.when(chip != base + k)
        def _():
            to_owner(lead, leads, k, lead_s, lead_r).start()

    @pl.when(chip == 0)
    def _():
        carry[...] = jnp.zeros_like(carry)

    def onward(g):
        return send(ahead.at[g], carry.at[place], carry_s.at[g], carry_r.at[place], 2 * g + core)

    @pl.when(owner)
    def _():
        gather[chip] = pair[place]
        value = None
        for g in range(chips - 1):

            @pl.when(chip != g)
            def _():
                from_chip(gather, g, pair_r).wait_recv()

            value = gather[g] if g == 0 else exact(a2, value) + gather[g]
            ahead[g + 1] = value

            @pl.when(chip != g + 1)
            def _():
                onward(g + 1).start()

            @pl.when(chip == g + 1)
            def _():
                carry[place] = ahead[g + 1]

    slot = 2 * place + core

    def share(d):
        to = lax.rem(me + d, n)
        return send(sq.at[slot], sq.at[slot], sq_s.at[to], sq_r.at[slot], to)

    @pl.when(owner)
    def _():
        priors[chip] = prior[place]
        leads[chip] = lead[place]
        squares = jnp.zeros((FP, lon), F32)
        for g in range(chips):

            @pl.when(chip != g)
            def _():
                from_chip(leads, g, lead_r).wait_recv()

            change = leads[g]
            if g > 0:

                @pl.when(chip != g)
                def _():
                    from_chip(priors, g, prior_r).wait_recv()

                first_change = ahead[g] - priors[g]
                squares = squares + first_change * first_change
                change = change + exact(a1, ahead[g])
            squares = squares + change * change
        total = lax.dot_general(
            jnp.ones((8, lon), F32), squares, (((1,), (1,)), ((), ())), precision=HIGHEST, preferred_element_type=F32
        )
        sq[slot] = jnp.concatenate([total, jnp.zeros((8, lon - FP), F32)], axis=1)
        each_other(n, lambda d: share(d).start())

    returns = []
    for k in range(half):

        @pl.when(jnp.logical_and(chip != 0, chip != base + k))
        def _():
            send(pair.at[0], carry.at[k], pair_s.at[0], carry_r.at[k], 2 * (base + k) + core).wait_recv()

        arrived = carry[k]
        n1 = exact(a1, arrived) + early[:, k * lon : (k + 1) * lon]
        n0 = jnp.where(chip == 0, prior[k], arrived)
        give[k] = jnp.where(upper, n1, n0)
        copy = send(give.at[k], back.at[k], back_s.at[k], back_r.at[k], mate)
        copy.start()
        returns.append(copy)
        keep[k] = jnp.where(upper, n0, n1)

    for k in range(half):
        new_ref[pl.ds(mine + k, fields, stride=rows), :] = keep[k, 0:fields]
    for k in range(half):
        returns[k].wait_recv()
        new_ref[pl.ds(half - mine + k, fields, stride=rows), :] = back[k, 0:fields]
    out = pltpu.make_async_copy(new_ref, new_hbm, store)
    out.start()

    for other in range(2 * half):
        of = 2 * (base + other // 2) + other % 2

        @pl.when(me != of)
        def _():
            send(sq.at[other], sq.at[other], sq_s.at[of], sq_r.at[other], of).wait_recv()


    everyone = jnp.sum(sq[...], axis=0)
    size_ref[...] = jnp.sqrt(everyone[0:1, 0:fields] / (n * cells) + 1e-06)

    @pl.when(owner)
    def _():
        each_other(n, lambda d: share(d).wait_send())


    for copy in [olds, to_mate] + returns:
        copy.wait_send()
    for k in range(half):

        @pl.when(jnp.logical_and(chip != base + k, chip != chips - 1))
        def _():
            to_owner(pair, gather, k, pair_s, pair_r).wait_send()

        @pl.when(chip != base + k)
        def _():
            to_owner(lead, leads, k, lead_s, lead_r).wait_send()

        @pl.when(jnp.logical_and(chip != base + k, chip != 0))
        def _():
            to_owner(prior, priors, k, prior_s, prior_r).wait_send()

    @pl.when(owner)
    def _():
        for g in range(1, chips):

            @pl.when(chip != g)
            def _():
                onward(g).wait_send()

    out.wait()


def per_device(n, old_start, weight_in, weight_mid, weight_out, tendency):
    _, fields, rows, lon = old_start.shape
    ch = weight_in.shape[1]
    cells = rows * lon
    half = rows // 2
    wide = lon + cells + lon
    chips = n // 2
    flat = old_start.reshape(fields * rows, lon)
    args = (flat, weight_in, weight_mid, weight_out, tendency)
    hbm = pl.BlockSpec(memory_space=pl.ANY)
    dma = pltpu.SemaphoreType.DMA

    def state(*lead):
        return pltpu.VMEM(lead + (FP, lon), F32)

    new, size = pl.pallas_call(
        functools.partial(program, n),
        out_shape=(jax.ShapeDtypeStruct(flat.shape, F32), jax.ShapeDtypeStruct((1, fields), F32)),
        in_specs=[hbm] * 5,
        out_specs=(hbm, pl.BlockSpec(memory_space=pltpu.VMEM)),
        scratch_shapes=[pltpu.VMEM(a.shape, a.dtype) for a in args]
        + [
            pltpu.VMEM(flat.shape, F32),
            pltpu.VMEM((rows, FK, lon), F32),
            pltpu.VMEM((FP, 128), F32),
            pltpu.VMEM((640, ch), F32),
            pltpu.VMEM((3, 256, ch), BF16),
            pltpu.VMEM((3, 3 * FK, ch), BF16),
            pltpu.VMEM((wide, 256), BF16),
            pltpu.VMEM((wide, 3 * ch), BF16),
            pltpu.VMEM((wide, ch), BF16),
            state(rows),
            state(half),
            state(rows),
            state(half),
            state(half),
            state(chips),
            state(half),
            state(chips),
            state(half),
            state(half),
            state(half),
            pltpu.VMEM((2 * half, 8, lon), F32),
            state(half),
            state(chips),
            state(half),
            state(chips),
            dma((half,)),
            dma((chips,)),
            dma((half,)),
            dma((chips,)),
            dma((5,)),
            dma,
            dma,
            dma,
            dma,
            dma,
            dma((half,)),
            dma((chips,)),
            dma((chips,)),
            dma((half,)),
            dma((half,)),
            dma((half,)),
            dma((n,)),
            dma((2 * half,)),
        ],
        compiler_params=pltpu.CompilerParams(
            collective_id=0, has_side_effects=True, vmem_limit_bytes=54900 * 2**10
        ),
        name="parareal",
    )(*args)
    return (new.reshape(old_start.shape), size.reshape(fields))


def solution(mesh):
    in_specs = (P(("grp", "tm"), None, None, None), P(), P(), P(), P())
    out_specs = (P(("grp", "tm"), None, None, None), P("grp"))
    return jax.shard_map(
        functools.partial(per_device, mesh.shape["tm"]),
        mesh=mesh, in_specs=in_specs, out_specs=out_specs, check_vma=False,
    )
```

```python
import functools

import jax
import jax.numpy as jnp
from jax import lax
from jax.experimental import pallas as pl
from jax.experimental.pallas import tpu as pltpu
from jax.sharding import PartitionSpec as P

FINE = 2
DAMPING = 0.995
MESH = pl.DeviceIdType.MESH
HIGHEST = lax.Precision.HIGHEST
F32 = jnp.float32
BF16 = jnp.bfloat16

FP = 72
FK = 80
CHUNK = 256


def exact(a, b):
    return jnp.dot(a, b, precision=HIGHEST, preferred_element_type=F32)


def silu(x):
    return 0.5 * x * (1.0 + jnp.tanh(0.5 * x))


def coarse_matrix(ten_ref, mat):
    fields = ten_ref.shape[0]
    mat[...] = jnp.zeros_like(mat)
    mat[0:fields, 0:fields] = ten_ref[...]
    across = lax.broadcasted_iota(jnp.int32, (FP, FP), 0)
    down = lax.broadcasted_iota(jnp.int32, (FP, FP), 1)
    return mat[:, 0:FP] + jnp.where(across == down, DAMPING, 0.0).astype(F32)


def each_other(n, act):
    if n <= 32:
        for d in range(1, n):
            act(d)
    else:
        pl.loop(1, n)(act)


def program(n, u_hbm, win_hbm, wmid_hbm, wout_hbm, ten_hbm, new_ref, size_ref,
            u_ref, win_ref, wmid_ref, wout_ref, ten_ref,
            cur, mat, wtall, wi, wo, xt, hcat, h2,
            old, old_mate, force, near, pair, gather, carry, ahead, give, keep, back, sq,
            prior, priors, lead, leads, prior_s, prior_r, lead_s, lead_r, load, old_s, old_r, near_s, near_r, pair_s, pair_r, carry_s, carry_r, back_s, back_r, sq_s, sq_r):
    fields = ten_ref.shape[0]
    ch = win_ref.shape[1]
    rows, _, lon = cur.shape
    cells = rows * lon
    half = rows // 2
    chips = n // 2
    me = lax.axis_index("tm")
    core = lax.rem(me, 2)
    chip = me // 2
    mate = me + 1 - 2 * core
    upper = core == 0

    loads = [
        pltpu.make_async_copy(src, dst, load.at[k])
        for k, (src, dst) in enumerate(
            ((win_hbm, win_ref), (u_hbm, u_ref), (wout_hbm, wout_ref), (ten_hbm, ten_ref), (wmid_hbm, wmid_ref))
        )
    ]
    for copy in loads:
        copy.start()
    barrier = pltpu.get_barrier_semaphore()

    def greet(d):
        pl.semaphore_signal(barrier, inc=1, device_id={"tm": lax.rem(me + d, n)}, device_id_type=MESH)

    each_other(n, greet)

    def send(src, dst, sent, got, to):
        return pltpu.make_async_remote_copy(
            src_ref=src, dst_ref=dst, send_sem=sent, recv_sem=got, device_id={"tm": to}, device_id_type=MESH
        )

    mine = core * half
    base = chips // 2 - half // 2
    place = chip - base
    owner = jnp.logical_and(place >= 0, place < half)
    place = jnp.clip(place, 0, half - 1)

    def to_owner(src, dst, k, sent, got):
        return send(src.at[k], dst.at[chip], sent.at[k], got.at[chip], 2 * (base + k) + core)

    def from_chip(dst, g, got):
        return send(pair.at[0], dst.at[g], pair_s.at[0], got.at[g], 2 * g + core)

    wi[...] = jnp.zeros_like(wi)
    wo[...] = jnp.zeros_like(wo)
    cur[...] = jnp.zeros_like(cur)
    for pad in (xt, hcat, h2):
        pad[0:lon] = jnp.zeros((lon, pad.shape[1]), BF16)
        pad[lon + cells :] = jnp.zeros((lon, pad.shape[1]), BF16)
    wtall[9 * fields :] = jnp.zeros((wtall.shape[0] - 9 * fields, ch), F32)
    loads[0].wait()
    wtall[0 : 9 * fields] = win_ref[...].astype(F32)
    for t in range(9):
        a, b = divmod(t, 3)
        wi[a, b * FK : (b + 1) * FK] = wtall[t * fields : t * fields + FK].astype(BF16)
    loads[1].wait()
    for r in range(rows):
        cur[r, 0:fields] = u_ref[pl.ds(r, fields, stride=rows), :]
        old[r] = cur[r, 0:FP]
    loads[2].wait()
    for t in range(9):
        a, b = divmod(t, 3)
        wo[a, b * FK : b * FK + fields] = wout_ref[:, t * ch : (t + 1) * ch]
    loads[3].wait()
    a1 = coarse_matrix(ten_ref, mat)
    a2 = exact(a1, a1)
    moved = jnp.where(me == 0, 0.0, 1.0).astype(F32)

    for step in range(FINE):
        for r in range(rows):
            x = cur[r]
            wide = jnp.concatenate(
                [pltpu.roll(x, 1, 1), x, pltpu.roll(x, lon - 1, 1), jnp.zeros((xt.shape[1] - 3 * FK, lon), F32)], axis=0
            )
            xt[(r + 1) * lon : (r + 2) * lon] = wide.T.astype(BF16)
        for m in range(0, cells, CHUNK):
            wide = silu(
                sum(
                    jnp.dot(xt[m + a * lon : m + a * lon + CHUNK], wi[a], preferred_element_type=F32)
                    for a in range(3)
                )
            )
            for k in range(0, CHUNK, lon):
                h = wide[k : k + lon]
                here = slice(m + k + lon, m + k + 2 * lon)
                hcat[here, 0:ch] = pltpu.roll(h, 1, 0).astype(BF16)
                hcat[here, ch : 2 * ch] = h.astype(BF16)
                hcat[here, 2 * ch : 3 * ch] = pltpu.roll(h, lon - 1, 0).astype(BF16)
        if step == 0:
            loads[4].wait()
        if step == FINE - 1:
            olds.wait_recv()
            for k in range(half):
                prior[k] = jnp.where(upper, old[mine + k], old_mate[k])

                @pl.when(jnp.logical_and(chip != base + k, chip != 0))
                def _():
                    to_owner(prior, priors, k, prior_s, prior_r).start()

        for m in range(0, cells, CHUNK):
            h2[m + lon : m + lon + CHUNK] = silu(
                sum(
                    jnp.dot(
                        hcat[m + a * lon : m + a * lon + CHUNK],
                        wmid_ref[a * 3 * ch : (a + 1) * 3 * ch],
                        preferred_element_type=F32,
                    )
                    for a in range(3)
                )
            ).astype(BF16)
        for part in (1 - core, core):
            first = part * half
            y = sum(
                lax.dot_general(
                    wo[a],
                    h2[pl.ds(pl.multiple_of((first + a) * lon, lon), half * lon), :],
                    (((1,), (1,)), ((), ())),
                    preferred_element_type=F32,
                )
                for a in range(3)
            )
            for k in range(half):
                piece = y[:, k * lon : (k + 1) * lon]
                cur[first + k] = (
                    cur[first + k]
                    + piece[FK : 2 * FK]
                    + pltpu.roll(piece[0:FK], 1, 1)
                    + pltpu.roll(piece[2 * FK : 3 * FK], lon - 1, 1)
                )
            if step == FINE - 1:
                before = jnp.concatenate([old[first + k] for k in range(half)], axis=1)
                mapped = moved * exact(a1, before)
                for k in range(half):
                    force[first + k] = cur[first + k, 0:FP] - mapped[:, k * lon : (k + 1) * lon]
                if part is not core:
                    to_mate = send(force.at[pl.ds(first, half)], near, near_s, near_r, mate)
                    to_mate.start()
        if step == 0:
            pl.semaphore_wait(barrier, n - 1)
            olds = send(old.at[pl.ds((1 - core) * half, half)], old_mate, old_s, old_r, mate)
            olds.start()

    to_mate.wait_recv()
    early = jnp.concatenate([jnp.where(upper, force[mine + k], near[k]) for k in range(half)], axis=1)
    mixed = exact(a1, early)
    for k in range(half):
        late = jnp.where(upper, near[k], force[mine + k])
        pair[k] = mixed[:, k * lon : (k + 1) * lon] + late

        @pl.when(jnp.logical_and(chip != base + k, chip != chips - 1))
        def _():
            to_owner(pair, gather, k, pair_s, pair_r).start()

    for k in range(half):
        lead[k] = early[:, k * lon : (k + 1) * lon] - jnp.where(upper, old_mate[k], old[mine + k])

        @pl.when(chip != base + k)
        def _():
            to_owner(lead, leads, k, lead_s, lead_r).start()

    @pl.when(chip == 0)
    def _():
        carry[...] = jnp.zeros_like(carry)

    def onward(g):
        return send(ahead.at[g], carry.at[place], carry_s.at[g], carry_r.at[place], 2 * g + core)

    @pl.when(owner)
    def _():
        gather[chip] = pair[place]
        value = None
        for g in range(chips - 1):

            @pl.when(chip != g)
            def _():
                from_chip(gather, g, pair_r).wait_recv()

            value = gather[g] if g == 0 else exact(a2, value) + gather[g]
            ahead[g + 1] = value

            @pl.when(chip != g + 1)
            def _():
                onward(g + 1).start()

            @pl.when(chip == g + 1)
            def _():
                carry[place] = ahead[g + 1]

    slot = 2 * place + core

    def share(d):
        to = lax.rem(me + d, n)
        return send(sq.at[slot], sq.at[slot], sq_s.at[to], sq_r.at[slot], to)

    @pl.when(owner)
    def _():
        priors[chip] = prior[place]
        leads[chip] = lead[place]
        squares = jnp.zeros((FP, lon), F32)
        for g in range(chips):

            @pl.when(chip != g)
            def _():
                from_chip(leads, g, lead_r).wait_recv()

            change = leads[g]
            if g > 0:

                @pl.when(chip != g)
                def _():
                    from_chip(priors, g, prior_r).wait_recv()

                first_change = ahead[g] - priors[g]
                squares = squares + first_change * first_change
                change = change + exact(a1, ahead[g])
            squares = squares + change * change
        total = lax.dot_general(
            jnp.ones((8, lon), F32), squares, (((1,), (1,)), ((), ())), precision=HIGHEST, preferred_element_type=F32
        )
        sq[slot] = jnp.concatenate([total, jnp.zeros((8, lon - FP), F32)], axis=1)
        each_other(n, lambda d: share(d).start())

    returns = []
    for k in range(half):

        @pl.when(jnp.logical_and(chip != 0, chip != base + k))
        def _():
            send(pair.at[0], carry.at[k], pair_s.at[0], carry_r.at[k], 2 * (base + k) + core).wait_recv()

        arrived = carry[k]
        n1 = exact(a1, arrived) + early[:, k * lon : (k + 1) * lon]
        n0 = jnp.where(chip == 0, prior[k], arrived)
        give[k] = jnp.where(upper, n1, n0)
        copy = send(give.at[k], back.at[k], back_s.at[k], back_r.at[k], mate)
        copy.start()
        returns.append(copy)
        keep[k] = jnp.where(upper, n0, n1)

    for k in range(half):
        new_ref[pl.ds(mine + k, fields, stride=rows), :] = keep[k, 0:fields]
    for k in range(half):
        returns[k].wait_recv()
        new_ref[pl.ds(half - mine + k, fields, stride=rows), :] = back[k, 0:fields]

    for other in range(2 * half):
        of = 2 * (base + other // 2) + other % 2

        @pl.when(me != of)
        def _():
            send(sq.at[other], sq.at[other], sq_s.at[of], sq_r.at[other], of).wait_recv()


    everyone = jnp.sum(sq[...], axis=0)
    size_ref[...] = jnp.sqrt(everyone[0:1, 0:fields] / (n * cells) + 1e-06)

    @pl.when(owner)
    def _():
        each_other(n, lambda d: share(d).wait_send())


    for copy in [olds, to_mate] + returns:
        copy.wait_send()
    for k in range(half):

        @pl.when(jnp.logical_and(chip != base + k, chip != chips - 1))
        def _():
            to_owner(pair, gather, k, pair_s, pair_r).wait_send()

        @pl.when(chip != base + k)
        def _():
            to_owner(lead, leads, k, lead_s, lead_r).wait_send()

        @pl.when(jnp.logical_and(chip != base + k, chip != 0))
        def _():
            to_owner(prior, priors, k, prior_s, prior_r).wait_send()

    @pl.when(owner)
    def _():
        for g in range(1, chips):

            @pl.when(chip != g)
            def _():
                onward(g).wait_send()


def per_device(n, old_start, weight_in, weight_mid, weight_out, tendency):
    _, fields, rows, lon = old_start.shape
    ch = weight_in.shape[1]
    cells = rows * lon
    half = rows // 2
    wide = lon + cells + lon
    chips = n // 2
    flat = old_start.reshape(fields * rows, lon)
    args = (flat, weight_in, weight_mid, weight_out, tendency)
    hbm = pl.BlockSpec(memory_space=pl.ANY)
    dma = pltpu.SemaphoreType.DMA

    def state(*lead):
        return pltpu.VMEM(lead + (FP, lon), F32)

    new, size = pl.pallas_call(
        functools.partial(program, n),
        out_shape=(jax.ShapeDtypeStruct(flat.shape, F32), jax.ShapeDtypeStruct((1, fields), F32)),
        in_specs=[hbm] * 5,
        out_specs=(pl.BlockSpec(memory_space=pltpu.VMEM),) * 2,
        scratch_shapes=[pltpu.VMEM(a.shape, a.dtype) for a in args]
        + [
            pltpu.VMEM((rows, FK, lon), F32),
            pltpu.VMEM((FP, 128), F32),
            pltpu.VMEM((640, ch), F32),
            pltpu.VMEM((3, 256, ch), BF16),
            pltpu.VMEM((3, 3 * FK, ch), BF16),
            pltpu.VMEM((wide, 256), BF16),
            pltpu.VMEM((wide, 3 * ch), BF16),
            pltpu.VMEM((wide, ch), BF16),
            state(rows),
            state(half),
            state(rows),
            state(half),
            state(half),
            state(chips),
            state(half),
            state(chips),
            state(half),
            state(half),
            state(half),
            pltpu.VMEM((2 * half, 8, lon), F32),
            state(half),
            state(chips),
            state(half),
            state(chips),
            dma((half,)),
            dma((chips,)),
            dma((half,)),
            dma((chips,)),
            dma((5,)),
            dma,
            dma,
            dma,
            dma,
            dma((half,)),
            dma((chips,)),
            dma((chips,)),
            dma((half,)),
            dma((half,)),
            dma((half,)),
            dma((n,)),
            dma((2 * half,)),
        ],
        compiler_params=pltpu.CompilerParams(
            collective_id=0, has_side_effects=True, vmem_limit_bytes=54900 * 2**10
        ),
        name="parareal",
    )(*args)
    return (new.reshape(old_start.shape), size.reshape(fields))


def solution(mesh):
    in_specs = (P(("grp", "tm"), None, None, None), P(), P(), P(), P())
    out_specs = (P(("grp", "tm"), None, None, None), P("grp"))
    return jax.shard_map(
        functools.partial(per_device, mesh.shape["tm"]),
        mesh=mesh, in_specs=in_specs, out_specs=out_specs, check_vma=False,
    )
```
